256 devices in a mesh: frames: 32 (over y, z), wshard: 8 (over x, core).
Axes of the slice: x: 4, y: 4, z: 8, core: 2. Of those that a mesh axis runs over, the one named last changes fastest.
Arguments:
- queries: bfloat16 [32, 2048, 5120], P('frames', None, 'wshard')
- keys: bfloat16 [32, 2048, 5120], P('frames', None, 'wshard')
- values: bfloat16 [32, 2048, 5120], P('frames', None, 'wshard'), may hold values from -6 to 6
- labels: int32 [40], P('wshard'), may hold values from 0 to 1, as said below
Outputs:
- attended: bfloat16 [32, 2048, 5120], P('frames', None, 'wshard')
The draws below stay inside these ranges and needn't reach their ends.
Inputs may be any that keep to these rules, and one draw needn't show every extreme that they name: `labels`: at most 3 of the 5 heads h * 5 to (h + 1) * 5 - 1 are temporal for each h, and some such group holds exactly 3.
All inputs are finite; a program needn't handle non-finite values.
Results may differ from the reference program's by a relative error of at most 0.011.
Values may be sent and summed in bfloat16 or wider, within the bound.
A program may use at most 128 MiB of HBM per device.

```python
import jax
import jax.numpy as jnp
from jax import lax

HEADS = 40
HD = 128
POS = 2048
FRAMES = 32
H_DEV = 5
TMAX = 3


def base_keys(key):
    return jax.random.normal(key, (FRAMES, POS, HEADS * HD), jnp.float32)


def draw_keys(key, part):
    return base_keys(key).astype(jnp.bfloat16)


def draw_queries(key, part):
    key = jax.random.fold_in(key, 7)
    fresh = jax.random.normal(key, (FRAMES, POS, HEADS * HD), jnp.float32)
    return fresh.astype(jnp.bfloat16)


def draw_labels(key, part):
    key = jax.random.fold_in(key, 3)
    groups = HEADS // H_DEV
    count_key, pick_key, perm_key = jax.random.split(key, 3)
    counts = jax.random.randint(count_key, (groups,), 0, TMAX + 1)
    forced = jax.random.randint(pick_key, (), 0, groups)
    counts = jnp.where(jnp.arange(groups) == forced, TMAX, counts)
    perm_keys = jax.random.split(perm_key, groups)
    ranks = jax.vmap(lambda one: jax.random.permutation(one, H_DEV))(perm_keys)
    return (ranks < counts[:, None]).astype(jnp.int32).reshape(HEADS)


def shard_levels(stream_key, shape, pieces, smallest, largest):
    def one(dim, parts):
        steps = jax.random.uniform(jax.random.fold_in(jax.random.fold_in(stream_key, 6), dim), (parts,), jnp.float32, smallest / len(pieces), largest / len(pieces))
        return jnp.repeat(jnp.exp(steps), shape[dim] // parts).reshape((-1,) + (1,) * (len(shape) - dim - 1))

    loudness = one(*pieces[0])
    for cut in pieces[1:]:
        loudness = loudness * one(*cut)
    return loudness


def centred(stream_key, extent, spread, reach, cuts=(), dtype=jnp.bfloat16):
    values = spread * jax.random.normal(stream_key, extent, jnp.float32)
    if cuts:
        values = values * shard_levels(stream_key, extent, cuts, -0.22, 0.18)
    return jnp.clip(values, -reach, reach).astype(dtype)


def setup_inputs(seed: int = 0) -> dict:
    streams_of = jax.random.split(jax.random.key(seed), 5)
    queries = draw_queries(jax.random.fold_in(streams_of[4], 71), 0)
    keys = draw_keys(jax.random.fold_in(streams_of[4], 71), 0)
    values = centred(streams_of[2], (FRAMES, POS, HEADS * HD), 1.0, 6.0, ((0, 32), (2, 8)))
    labels = draw_labels(jax.random.fold_in(streams_of[4], 71), 0)
    return dict(queries=queries, keys=keys, values=values, labels=labels)


def softmax_apply(scores, vals):
    top = jnp.max(scores, axis=-1, keepdims=True)
    expo = jnp.exp(scores - top)
    weights = (expo / jnp.sum(expo, axis=-1, keepdims=True)).astype(jnp.bfloat16)
    return weights, vals


def reference(queries, keys, values, labels):
    frame_count, pos_count, width = queries.shape
    scale = HD ** -0.5
    q_heads = jnp.moveaxis(queries.reshape(frame_count, pos_count, HEADS, HD), 2, 0)
    k_heads = jnp.moveaxis(keys.reshape(frame_count, pos_count, HEADS, HD), 2, 0)
    v_heads = jnp.moveaxis(values.reshape(frame_count, pos_count, HEADS, HD), 2, 0)

    def one_head(item):
        qh, kh, vh, label = item

        def spatial():
            def frame_attend(trio):
                qf, kf, vf = trio
                scores = jnp.dot(qf, kf.T, preferred_element_type=jnp.float32) * scale
                weights, vals = softmax_apply(scores, vf)
                return jnp.dot(weights, vals, preferred_element_type=jnp.float32).astype(jnp.bfloat16)
            return lax.map(frame_attend, (qh, kh, vh))

        def temporal():
            scores = jnp.einsum("fpd,gpd->pfg", qh.astype(jnp.float32), kh.astype(jnp.float32)) * scale
            weights, vals = softmax_apply(scores, vh)
            result = jnp.einsum("pfg,gpd->fpd", weights.astype(jnp.float32), vals.astype(jnp.float32))
            return result.astype(jnp.bfloat16)

        return lax.cond(label == 1, temporal, spatial)

    outputs = lax.map(one_head, (q_heads, k_heads, v_heads, labels))
    return jnp.moveaxis(outputs, 0, 2).reshape(frame_count, pos_count, width)
```

```python
import functools

import jax
import jax.numpy as jnp
from jax import lax
from jax.experimental import pallas as pl
from jax.experimental.pallas import tpu as pltpu
from jax.sharding import PartitionSpec as P

HD = 128
SLOTS = 3
GROUP = 16
ROWS = 256
COEF = HD ** (-0.5) * 1.4426950408889634
MESH = pl.DeviceIdType.MESH


def dot_t(a, b):
    return lax.dot_general(a, b, (((1,), (1,)), ((), ())), preferred_element_type=jnp.float32)


def attend(scores, vals):
    top = jnp.max(scores, axis=-1, keepdims=True)
    expo = jnp.exp2((scores - top) * COEF)
    total = jnp.sum(expo, axis=-1, keepdims=True)
    out = jnp.dot(expo.astype(jnp.bfloat16), vals, preferred_element_type=jnp.float32)
    return (out / total).astype(jnp.bfloat16)


def kernel(frames, heads, table, flags, q, k, v, out, send, recv, result, back, ssem, rsem, ssem2, rsem2):
    me = lax.axis_index("frames")
    wsh = lax.axis_index("wshard")
    pos = q.shape[0]
    part = pos // frames
    peers = frames - 1

    def peer(step):
        return lax.rem(me + step, frames)

    barrier = pltpu.get_barrier_semaphore()

    def greet(step, carry):
        pl.semaphore_signal(barrier, inc=1, device_id=(peer(step), wsh), device_id_type=MESH)
        return carry

    lax.fori_loop(1, frames, greet, 0)

    def pack(s):
        lanes = pl.ds(table[s] * HD, HD)
        for u, ref in enumerate((q, k, v)):
            send[s, :, u] = ref[:, lanes].reshape(frames, part, HD)
        recv[s, me] = send[s, me]

    def forward(s):
        def step(o, carry):
            to = peer(o)
            pltpu.make_async_remote_copy(
                src_ref=send.at[s, to],
                dst_ref=recv.at[s, me],
                send_sem=ssem.at[s],
                recv_sem=rsem.at[s],
                device_id=(to, wsh),
                device_id_type=MESH,
            ).start()
            return carry

        lax.fori_loop(1, frames, step, 0)

    def backward(s):
        def step(o, carry):
            to = peer(o)
            pltpu.make_async_remote_copy(
                src_ref=result.at[s, to],
                dst_ref=back.at[s, me],
                send_sem=ssem2.at[s],
                recv_sem=rsem2.at[s],
                device_id=(to, wsh),
                device_id_type=MESH,
            ).start()
            return carry

        lax.fori_loop(1, frames, step, 0)

    def wait_all(ref, s, sem):
        some = ref.at[s, pl.ds(0, peers)]
        pltpu.make_async_copy(some, some, sem.at[s]).wait()

    wide = frames * GROUP
    mask = lax.rem(lax.broadcasted_iota(jnp.int32, (wide, wide), 0), GROUP) == lax.rem(
        lax.broadcasted_iota(jnp.int32, (wide, wide), 1), GROUP
    )

    def temporal(s):
        def step(g, carry):
            rows = pl.ds(pl.multiple_of(g * GROUP, GROUP), GROUP)
            qg = recv[s, :, 0, rows, :].reshape(wide, HD)
            kg = recv[s, :, 1, rows, :].reshape(wide, HD)
            vg = recv[s, :, 2, rows, :].reshape(wide, HD)
            scores = jnp.where(mask, dot_t(qg, kg), -jnp.inf)
            result[s, :, rows, :] = attend(scores, vg).reshape(frames, GROUP, HD)
            return carry

        lax.fori_loop(0, part // GROUP, step, 0)
        back[s, me] = result[s, me]

    blocks = pos // ROWS

    def spatial(first, last):
        def step(i, carry):
            h, b = i // blocks, lax.rem(i, blocks)
            lanes = pl.ds(pl.multiple_of(h * HD, HD), HD)
            rows = pl.ds(pl.multiple_of(b * ROWS, ROWS), ROWS)
            out[rows, lanes] = attend(dot_t(q[rows, lanes], k[:, lanes]), v[:, lanes])
            return carry

        lax.fori_loop(first * blocks, last * blocks, step, 0)

    pack(0)
    pl.semaphore_wait(barrier, peers)
    forward(0)
    for s in range(1, SLOTS):
        pack(s)
        forward(s)
    cuts = (0, 2, 4, heads)
    for s in range(SLOTS):
        spatial(cuts[s], cuts[s + 1])
        wait_all(recv, s, rsem)
        temporal(s)
        backward(s)
    for s in range(SLOTS):
        wait_all(send, s, ssem)
        wait_all(result, s, ssem2)
        wait_all(back, s, rsem2)
    for h in range(heads):
        lanes = slice(h * HD, (h + 1) * HD)
        got = back[table[SLOTS + h]].reshape(pos, HD)
        out[:, lanes] = jnp.where(flags[h : h + 1, :] == 1, got, out[:, lanes])


def tables(labels):
    heads = labels.shape[0]
    slot_of = jnp.minimum(jnp.cumsum(labels) - labels, SLOTS - 1)
    slots = jnp.arange(SLOTS)[:, None]
    hit = (labels == 1) & (slot_of == slots)
    head_of = jnp.sum(jnp.where(hit, jnp.arange(heads), 0), axis=1)
    flags = jnp.broadcast_to(labels[:, None], (heads, HD))
    return jnp.concatenate([head_of, slot_of]).astype(jnp.int32), flags


def body(queries, keys, values, labels):
    _, pos, width = queries.shape
    heads = width // HD
    frames = lax.axis_size("frames")
    part = pos // frames
    vmem = pl.BlockSpec(memory_space=pltpu.VMEM)
    bf16 = jnp.bfloat16
    sems = pltpu.SemaphoreType.DMA((SLOTS,))
    out = pl.pallas_call(
        functools.partial(kernel, frames, heads),
        out_shape=jax.ShapeDtypeStruct((pos, width), bf16),
        in_specs=[pl.BlockSpec(memory_space=pltpu.SMEM), vmem, vmem, vmem, vmem],
        out_specs=vmem,
        scratch_shapes=[
            pltpu.VMEM((SLOTS, frames, 3, part, HD), bf16),
            pltpu.VMEM((SLOTS, frames, 3, part, HD), bf16),
            pltpu.VMEM((SLOTS, frames, part, HD), bf16),
            pltpu.VMEM((SLOTS, frames, part, HD), bf16),
            sems,
            sems,
            sems,
            sems,
        ],
        compiler_params=pltpu.CompilerParams(
            collective_id=0, has_side_effects=True, vmem_limit_bytes=60 << 20
        ),
        name="attention",
    )(*tables(labels), queries.reshape(pos, width), keys.reshape(pos, width), values.reshape(pos, width))
    return out.reshape(1, pos, width)


def solution(mesh):
    spec = P("frames", None, "wshard")
    return jax.shard_map(
        body,
        mesh=mesh,
        in_specs=(spec, spec, spec, P("wshard")),
        out_specs=spec,
        check_vma=False,
    )
```

```python
import functools

import jax
import jax.numpy as jnp
from jax import lax
from jax.experimental import pallas as pl
from jax.experimental.pallas import tpu as pltpu
from jax.sharding import PartitionSpec as P

HD = 128
SLOTS = 3
GROUP = 16
ROWS = 256
CHUNKS = 4
Y, Z, W = 4, 8, 8
COEF = HD ** (-0.5) * 1.4426950408889634
MESH = pl.DeviceIdType.MESH
SIZES = (8, 10, 12, 14, 16, 18, 20, 24)
HEAD, SLOT, SOURCE, PLACE, TABLE = 0, 8, 16, 48, 128


def dot_t(a, b):
    return lax.dot_general(a, b, (((1,), (1,)), ((), ())), preferred_element_type=jnp.float32)


def attend(scores, vals):
    top = jnp.max(scores, axis=-1, keepdims=True)
    expo = jnp.exp2((scores - top) * COEF)
    total = jnp.sum(expo, axis=-1, keepdims=True)
    out = jnp.dot(expo.astype(jnp.bfloat16), vals, preferred_element_type=jnp.float32)
    return (out / total).astype(jnp.bfloat16)


def share_kernel(heads, labels, every, mine, ssem, rsem):
    fr = lax.axis_index("frames")
    me = lax.axis_index("wshard")
    barrier = pltpu.get_barrier_semaphore()
    for o in range(1, W):
        to = (fr, lax.rem(me + o, W))
        pl.semaphore_signal(barrier, inc=1, device_id=to, device_id_type=MESH)
    lane = lax.broadcasted_iota(jnp.int32, (8, HD), 1)
    row = jnp.zeros((8, HD), jnp.int32)
    for h in range(heads):
        row += (lane == h).astype(jnp.int32) * labels[h]
    mine[...] = row
    every[me] = row
    pl.semaphore_wait(barrier, W - 1)
    for o in range(1, W):
        pltpu.make_async_remote_copy(
            src_ref=mine,
            dst_ref=every.at[me],
            send_sem=ssem,
            recv_sem=rsem,
            device_id=(fr, lax.rem(me + o, W)),
            device_id_type=MESH,
        ).start()
    some = every.at[pl.ds(0, W - 1)]
    pltpu.make_async_copy(some, some, ssem).wait()
    pltpu.make_async_copy(some, some, rsem).wait()


def share(labels):
    return pl.pallas_call(
        functools.partial(share_kernel, labels.shape[0]),
        out_shape=jax.ShapeDtypeStruct((W, 8, HD), jnp.int32),
        in_specs=[pl.BlockSpec(memory_space=pltpu.SMEM)],
        out_specs=pl.BlockSpec(memory_space=pltpu.VMEM),
        scratch_shapes=[
            pltpu.VMEM((8, HD), jnp.int32),
            pltpu.SemaphoreType.DMA,
            pltpu.SemaphoreType.DMA,
        ],
        compiler_params=pltpu.CompilerParams(collective_id=1, has_side_effects=True),
        name="share_labels",
    )(labels)


def table_kernel(heads, every, table, flags, which):
    me = lax.axis_index("wshard")
    for i in range(TABLE):
        table[i] = 0
    total = jnp.int32(0)
    for w in range(W):
        slot = jnp.int32(0)
        for h in range(heads):
            table[SOURCE + total] = w * SLOTS + slot
            table[PLACE + w * SLOTS + slot] = total
            label = every[w, 0, h]
            total += label
            slot += label
    last = total - 1
    for i in range(W * SLOTS):
        table[PLACE + i] = jnp.minimum(table[PLACE + i], last)
    for i in range(SLOTS, 32):
        table[SOURCE + i] = jnp.where(i < total, table[SOURCE + i], 0)
    branch = jnp.int32(0)
    for size in SIZES[:-1]:
        branch += (total > size).astype(jnp.int32)
    which[0] = branch
    slot = jnp.int32(0)
    for h in range(heads):
        label = every[me, 0, h]
        table[HEAD + slot] = h
        table[SLOT + h] = jnp.minimum(slot, SLOTS - 1)
        slot += label
        flags[h] = jnp.full((8, HD), label, jnp.int32)


def make_table(every, heads):
    return pl.pallas_call(
        functools.partial(table_kernel, heads),
        out_shape=(
            jax.ShapeDtypeStruct((TABLE,), jnp.int32),
            jax.ShapeDtypeStruct((heads, 8, HD), jnp.int32),
            jax.ShapeDtypeStruct((1,), jnp.int32),
        ),
        in_specs=[pl.BlockSpec(memory_space=pltpu.SMEM)],
        out_specs=(
            pl.BlockSpec(memory_space=pltpu.SMEM),
            pl.BlockSpec(memory_space=pltpu.VMEM),
            pl.BlockSpec(memory_space=pltpu.SMEM),
        ),
        name="make_table",
    )(every)


def kernel(n, heads, table, flags, q, k, v, out, *scratch):
    scratch = list(scratch)

    def take(count):
        some = scratch[:count]
        del scratch[:count]
        return some

    xsend, xrecv, ysend = take(CHUNKS), take(CHUNKS), take(CHUNKS)
    yrecv, result = take(2)
    yback, rsend, rback = take(CHUNKS), take(CHUNKS), take(CHUNKS)
    xs, xr, ys, yr, bs, br, rs, rr = scratch
    fr = lax.axis_index("frames")
    wsh = lax.axis_index("wshard")
    frames = Y * Z
    pos = q.shape[0]
    part = pos // (W * CHUNKS)
    half = n // 2
    my_y, my_z = fr // Z, lax.rem(fr, Z)
    my_class = lax.rem(my_y + my_z, CHUNKS)
    my_half = my_z // CHUNKS

    def peer(step):
        return lax.rem(fr + step, frames)

    barrier = pltpu.get_barrier_semaphore()

    def greet(step, carry):
        pl.semaphore_signal(barrier, inc=1, device_id=(peer(step), wsh), device_id_type=MESH)
        return carry

    for o in range(1, W):
        to = (fr, lax.rem(wsh + o, W))
        pl.semaphore_signal(barrier, inc=1, device_id=to, device_id_type=MESH)
    lax.fori_loop(1, frames, greet, 0)

    def remote(src, dst, send_sem, recv_sem, to):
        pltpu.make_async_remote_copy(
            src_ref=src,
            dst_ref=dst,
            send_sem=send_sem,
            recv_sem=recv_sem,
            device_id=to,
            device_id_type=MESH,
        ).start()

    def wait(some, sem):
        pltpu.make_async_copy(some, some, sem).wait()

    def pack(c):
        def step(w, carry):
            rows = pl.ds(pl.multiple_of((w * CHUNKS + c) * part, part), part)
            for s in range(SLOTS):
                lanes = pl.ds(table[HEAD + s] * HD, HD)
                for u, ref in enumerate((q, k, v)):
                    xsend[c][w, s, u] = ref[rows, lanes]
            return carry

        lax.fori_loop(0, W, step, 0)

    def across(src, dst, send_sem, recv_sem):
        mine = dst.at[wsh] if dst.shape[0] == W else dst.at[pl.ds(wsh * SLOTS, SLOTS)]
        pltpu.make_async_copy(src.at[wsh], mine, recv_sem).start()
        for o in range(1, W):
            to = lax.rem(wsh + o, W)
            remote(src.at[to], mine, send_sem, recv_sem, (fr, to))

    def compact(c):
        def step(i, carry):
            source = table[SOURCE + i]
            block = xrecv[c][source]
            for y in range(Y):
                ysend[c][y, i] = block[:, y * GROUP : (y + 1) * GROUP]
            return carry

        lax.fori_loop(0, n, step, 0)

    def forward(c):
        def step(e, carry):
            e = lax.rem(e + fr, 8)
            y, b = e // 2, lax.rem(e, 2)
            to = y * Z + lax.rem(c + CHUNKS - y, CHUNKS) + CHUNKS * b
            src = ysend[c].at[y, pl.ds(b * half, half)]

            @pl.when(to == fr)
            def _():
                pltpu.make_async_copy(src, yrecv.at[fr], yr).start()

            @pl.when(to != fr)
            def _():
                remote(src, yrecv.at[fr], ys, yr, (to, wsh))

            return carry

        lax.fori_loop(0, 2 * Y, step, 0)

    wide = frames * GROUP
    mask = lax.rem(lax.broadcasted_iota(jnp.int32, (wide, wide), 0), GROUP) == lax.rem(
        lax.broadcasted_iota(jnp.int32, (wide, wide), 1), GROUP
    )

    def temporal():
        def step(j, carry):
            qg = yrecv[:, j, 0].reshape(wide, HD)
            kg = yrecv[:, j, 1].reshape(wide, HD)
            vg = yrecv[:, j, 2].reshape(wide, HD)
            scores = jnp.where(mask, dot_t(qg, kg), -jnp.inf)
            result[:, j] = attend(scores, vg).reshape(frames, GROUP, HD)
            return carry

        lax.fori_loop(0, half, step, 0)

    def backward():
        for c in range(CHUNKS):

            @pl.when(my_class == c)
            def _():
                dst = yback[c].at[my_y, pl.ds(my_half * half, half)]
                pltpu.make_async_copy(result.at[fr], dst, br.at[c]).start()

                def step(o, carry):
                    to = peer(o)
                    remote(result.at[to], dst, bs, br.at[c], (to, wsh))
                    return carry

                lax.fori_loop(1, frames, step, 0)

    def unpack(c):
        def step(w, carry):
            for s in range(SLOTS):
                place = table[PLACE + w * SLOTS + s]
                rsend[c][w, s] = yback[c][:, place].reshape(part, HD)
            return carry

        lax.fori_loop(0, W, step, 0)

    blocks = pos // ROWS

    def spatial(first, last):
        def step(i, carry):
            h, b = i // blocks, lax.rem(i, blocks)
            lanes = pl.ds(pl.multiple_of(h * HD, HD), HD)
            rows = pl.ds(pl.multiple_of(b * ROWS, ROWS), ROWS)
            out[rows, lanes] = attend(dot_t(q[rows, lanes], k[:, lanes]), v[:, lanes])
            return carry

        lax.fori_loop(first, last, step, 0)

    def give_back(c):
        wait(yback[c], br.at[c])
        unpack(c)
        across(rsend[c], rback[c], rs.at[c], rr.at[c])

    def merge(c):
        wait(rback[c], rr.at[c])

        def step(w, carry):
            rows = pl.ds(pl.multiple_of((w * CHUNKS + c) * part, part), part)
            for h in range(heads):
                lanes = slice(h * HD, (h + 1) * HD)
                got = rback[c][w, table[SLOT + h]]
                out[rows, lanes] = jnp.where(flags[h, 0:1, :] == 1, got, out[rows, lanes])
            return carry

        lax.fori_loop(0, W, step, 0)

    fill = heads * blocks // (CHUNKS + 1)

    def stage(st, carry):
        spatial(st * fill, (st + 1) * fill)
        for c in range(CHUNKS):

            @pl.when(st == c)
            def _():
                wait(xrecv[c], xr.at[c])
                compact(c)
                forward(c)

        @pl.when(st == CHUNKS)
        def _():
            give_back(0)
            give_back(1)

        @pl.when(my_class == st - 1)
        def _():
            wait(yrecv, yr)
            temporal()
            backward()

        return carry

    pack(0)
    pl.semaphore_wait(barrier, frames + W - 2)
    for c in range(CHUNKS):
        if c:
            pack(c)
        across(xsend[c], xrecv[c], xs.at[c], xr.at[c])
    lax.fori_loop(0, CHUNKS + 1, stage, 0)
    give_back(2)
    merge(0)
    merge(1)
    give_back(3)
    merge(2)
    merge(3)
    for c in range(CHUNKS):
        wait(xsend[c].at[pl.ds(0, W - 1)], xs.at[c])
        wait(rsend[c].at[pl.ds(0, W - 1)], rs.at[c])
    wait(yrecv.at[pl.ds(0, frames - 1)], ys)
    wait(result.at[pl.ds(0, frames - 1)], bs)


def attention(n, index, table, flags, q, k, v):
    pos, width = q.shape
    heads = width // HD
    frames = Y * Z
    part = pos // (W * CHUNKS)
    half = n // 2
    vmem = pl.BlockSpec(memory_space=pltpu.VMEM)

    def buffers(count, *shape):
        return [pltpu.VMEM(shape, jnp.bfloat16)] * count

    one, each = pltpu.SemaphoreType.DMA, pltpu.SemaphoreType.DMA((CHUNKS,))
    return pl.pallas_call(
        functools.partial(kernel, n, heads),
        out_shape=jax.ShapeDtypeStruct((pos, width), jnp.bfloat16),
        in_specs=[pl.BlockSpec(memory_space=pltpu.SMEM), vmem, vmem, vmem, vmem],
        out_specs=vmem,
        scratch_shapes=[
            *buffers(CHUNKS, W, SLOTS, 3, part, HD),
            *buffers(CHUNKS, W * SLOTS, 3, part, HD),
            *buffers(CHUNKS, Y, n, 3, GROUP, HD),
            *buffers(1, frames, half, 3, GROUP, HD),
            *buffers(1, frames, half, GROUP, HD),
            *buffers(CHUNKS, Y, n, GROUP, HD),
            *buffers(CHUNKS, W, SLOTS, part, HD),
            *buffers(CHUNKS, W, SLOTS, part, HD),
            each,
            each,
            one,
            one,
            one,
            each,
            each,
            each,
        ],
        compiler_params=pltpu.CompilerParams(
            collective_id=2 + index, has_side_effects=True, vmem_limit_bytes=60 << 20
        ),
        name=f"attention_{n}",
    )(table, flags, q, k, v)


def body(queries, keys, values, labels):
    _, pos, width = queries.shape
    heads = width // HD
    table, flags, which = make_table(share(labels), heads)
    branches = [functools.partial(attention, n, i) for i, n in enumerate(SIZES)]
    q, k, v = (a.reshape(pos, width) for a in (queries, keys, values))
    out = lax.switch(which.reshape(()), branches, table, flags, q, k, v)
    return out.reshape(1, pos, width)


def solution(mesh):
    spec = P("frames", None, "wshard")
    return jax.shard_map(
        body,
        mesh=mesh,
        in_specs=(spec, spec, spec, P("wshard")),
        out_specs=spec,
        check_vma=False,
    )
```

```python
import functools

import jax
import jax.numpy as jnp
from jax import lax
from jax.experimental import pallas as pl
from jax.experimental.pallas import tpu as pltpu
from jax.sharding import PartitionSpec as P

HD = 128
SLOTS = 3
GROUP = 16
ROWS = 256
CHUNKS = 4
Y, Z, W = 4, 8, 8
COEF = HD ** (-0.5) * 1.4426950408889634
MESH = pl.DeviceIdType.MESH
SIZES = (10, 12, 14, 16)
PIECES = ((0, 0, 1), (0, 1, 2), (0, 2, 3), (1, 0, 3), (2, 0, 3), (3, 0, 3))
COUNT = len(PIECES)
HEAD, SLOT, SOURCE, PLACE, TABLE = 0, 8, 16, 48, 128


def dot_t(a, b):
    return lax.dot_general(a, b, (((1,), (1,)), ((), ())), preferred_element_type=jnp.float32)


def attend(scores, vals):
    top = jnp.max(scores, axis=-1, keepdims=True)
    expo = jnp.exp2((scores - top) * COEF)
    total = jnp.sum(expo, axis=-1, keepdims=True)
    out = jnp.dot(expo.astype(jnp.bfloat16), vals, preferred_element_type=jnp.float32)
    return (out / total).astype(jnp.bfloat16)


def share_kernel(heads, labels, every, mine, ssem, rsem):
    fr = lax.axis_index("frames")
    me = lax.axis_index("wshard")
    barrier = pltpu.get_barrier_semaphore()
    for o in range(1, W):
        to = (fr, lax.rem(me + o, W))
        pl.semaphore_signal(barrier, inc=1, device_id=to, device_id_type=MESH)
    lane = lax.broadcasted_iota(jnp.int32, (8, HD), 1)
    row = jnp.zeros((8, HD), jnp.int32)
    for h in range(heads):
        row += (lane == h).astype(jnp.int32) * labels[h]
    mine[...] = row
    every[me] = row
    pl.semaphore_wait(barrier, W - 1)
    for o in range(1, W):
        pltpu.make_async_remote_copy(
            src_ref=mine,
            dst_ref=every.at[me],
            send_sem=ssem,
            recv_sem=rsem,
            device_id=(fr, lax.rem(me + o, W)),
            device_id_type=MESH,
        ).start()
    some = every.at[pl.ds(0, W - 1)]
    pltpu.make_async_copy(some, some, ssem).wait()
    pltpu.make_async_copy(some, some, rsem).wait()


def share(labels):
    return pl.pallas_call(
        functools.partial(share_kernel, labels.shape[0]),
        out_shape=jax.ShapeDtypeStruct((W, 8, HD), jnp.int32),
        in_specs=[pl.BlockSpec(memory_space=pltpu.SMEM)],
        out_specs=pl.BlockSpec(memory_space=pltpu.VMEM),
        scratch_shapes=[
            pltpu.VMEM((8, HD), jnp.int32),
            pltpu.SemaphoreType.DMA,
            pltpu.SemaphoreType.DMA,
        ],
        compiler_params=pltpu.CompilerParams(collective_id=1, has_side_effects=True),
        name="share_labels",
    )(labels)


def table_kernel(heads, every, table, flags, which):
    me = lax.axis_index("wshard")
    for i in range(TABLE):
        table[i] = 0
    total = jnp.int32(0)
    for w in range(W):
        slot = jnp.int32(0)
        for h in range(heads):
            table[SOURCE + total] = w * SLOTS + slot
            table[PLACE + w * SLOTS + slot] = total
            label = every[w, 0, h]
            total += label
            slot += label
    last = total - 1
    for i in range(W * SLOTS):
        table[PLACE + i] = jnp.minimum(table[PLACE + i], last)
    for i in range(SLOTS, 32):
        table[SOURCE + i] = jnp.where(i < total, table[SOURCE + i], 0)
    branch = jnp.int32(0)
    for size in SIZES:
        branch += (total > size).astype(jnp.int32)
    which[0] = branch
    slot = jnp.int32(0)
    for h in range(heads):
        label = every[me, 0, h]
        table[HEAD + slot] = h
        table[SLOT + h] = jnp.minimum(slot, SLOTS - 1)
        slot += label
        flags[h] = jnp.full((8, HD), label, jnp.int32)


def make_table(every, heads):
    return pl.pallas_call(
        functools.partial(table_kernel, heads),
        out_shape=(
            jax.ShapeDtypeStruct((TABLE,), jnp.int32),
            jax.ShapeDtypeStruct((heads, 8, HD), jnp.int32),
            jax.ShapeDtypeStruct((1,), jnp.int32),
        ),
        in_specs=[pl.BlockSpec(memory_space=pltpu.SMEM)],
        out_specs=(
            pl.BlockSpec(memory_space=pltpu.SMEM),
            pl.BlockSpec(memory_space=pltpu.VMEM),
            pl.BlockSpec(memory_space=pltpu.SMEM),
        ),
        name="make_table",
    )(every)


def kernel(n, heads, table, flags, q, k, v, out, *scratch):
    scratch = list(scratch)

    def take(count):
        some = scratch[:count]
        del scratch[:count]
        return some

    xsend, xrecv, ysend = take(COUNT), take(COUNT), take(COUNT)
    yrecv, result = take(2)
    yback, rsend, rback = take(CHUNKS), take(CHUNKS), take(CHUNKS)
    xs, xr, ys, yr, bs, br, rs, rr = scratch
    fr = lax.axis_index("frames")
    wsh = lax.axis_index("wshard")
    frames = Y * Z
    pos = q.shape[0]
    part = pos // (W * CHUNKS)
    half = n // 2
    my_y, my_z = fr // Z, lax.rem(fr, Z)
    my_class = lax.rem(my_y + my_z, CHUNKS)
    my_half = my_z // CHUNKS

    def peer(step):
        return lax.rem(fr + step, frames)

    barrier = pltpu.get_barrier_semaphore()

    def greet(step, carry):
        pl.semaphore_signal(barrier, inc=1, device_id=(peer(step), wsh), device_id_type=MESH)
        return carry

    for o in range(1, W):
        to = (fr, lax.rem(wsh + o, W))
        pl.semaphore_signal(barrier, inc=1, device_id=to, device_id_type=MESH)
    lax.fori_loop(1, frames, greet, 0)

    def remote(src, dst, send_sem, recv_sem, to):
        pltpu.make_async_remote_copy(
            src_ref=src,
            dst_ref=dst,
            send_sem=send_sem,
            recv_sem=recv_sem,
            device_id=to,
            device_id_type=MESH,
        ).start()

    def wait(some, sem):
        pltpu.make_async_copy(some, some, sem).wait()

    def pack(p):
        c, first, last = PIECES[p]
        cls = lax.rem(my_class + c, CHUNKS)

        def step(w, carry):
            rows = pl.ds(pl.multiple_of((w * CHUNKS + cls) * part, part), part)
            for s in range(SLOTS):
                lanes = pl.ds(table[HEAD + s] * HD, HD)
                for u in range(first, last):
                    xsend[p][w, s, u - first] = (q, k, v)[u][rows, lanes]
            return carry

        lax.fori_loop(0, W, step, 0)

    def across(src, dst, send_sem, recv_sem):
        mine = dst.at[wsh] if dst.shape[0] == W else dst.at[pl.ds(wsh * SLOTS, SLOTS)]
        pltpu.make_async_copy(src.at[wsh], mine, recv_sem).start()
        for o in range(1, W):
            to = lax.rem(wsh + o, W)
            remote(src.at[to], mine, send_sem, recv_sem, (fr, to))

    def compact(p):
        def step(i, carry):
            source = table[SOURCE + i]
            block = xrecv[p][source]
            for y in range(Y):
                ysend[p][y, i] = block[:, y * GROUP : (y + 1) * GROUP]
            return carry

        lax.fori_loop(0, n, step, 0)

    def forward(p):
        c, first, last = PIECES[p]
        cls = lax.rem(my_class + c, CHUNKS)

        def step(e, carry):
            y = lax.rem(e // 2 + my_y, Y)
            b = lax.rem(e + my_half, 2)
            to = y * Z + lax.rem(cls + CHUNKS - y, CHUNKS) + CHUNKS * b
            src = ysend[p].at[y, pl.ds(b * half, half)]
            dst = yrecv.at[fr, :, pl.ds(first, last - first)]

            @pl.when(to == fr)
            def _():
                pltpu.make_async_copy(src, dst, yr).start()

            @pl.when(to != fr)
            def _():
                remote(src, dst, ys, yr, (to, wsh))

            return carry

        lax.fori_loop(0, 2 * Y, step, 0)

    wide = frames * GROUP
    mask = lax.rem(lax.broadcasted_iota(jnp.int32, (wide, wide), 0), GROUP) == lax.rem(
        lax.broadcasted_iota(jnp.int32, (wide, wide), 1), GROUP
    )

    def temporal():
        def step(j, carry):
            qg = yrecv[:, j, 0].reshape(wide, HD)
            kg = yrecv[:, j, 1].reshape(wide, HD)
            vg = yrecv[:, j, 2].reshape(wide, HD)
            scores = jnp.where(mask, dot_t(qg, kg), -jnp.inf)
            result[:, j] = attend(scores, vg).reshape(frames, GROUP, HD)
            return carry

        lax.fori_loop(0, half, step, 0)

    def backward():
        for c in range(CHUNKS):
            dst = yback[c].at[my_y, pl.ds(my_half * half, half)]
            cls = lax.rem(my_class + c, CHUNKS)

            def step(e, carry):
                y = lax.rem(e // 2 + my_y, Y)
                b = lax.rem(e + my_half, 2)
                to = y * Z + lax.rem(cls + CHUNKS - y, CHUNKS) + CHUNKS * b

                @pl.when(to == fr)
                def _():
                    pltpu.make_async_copy(result.at[fr], dst, br.at[c]).start()

                @pl.when(to != fr)
                def _():
                    remote(result.at[to], dst, bs, br.at[c], (to, wsh))

                return carry

            lax.fori_loop(0, 2 * Y, step, 0)

    def unpack(c):
        def step(w, carry):
            for s in range(SLOTS):
                place = table[PLACE + w * SLOTS + s]
                rsend[c][w, s] = yback[c][:, place].reshape(part, HD)
            return carry

        lax.fori_loop(0, W, step, 0)

    blocks = pos // ROWS

    def spatial(first, last):
        def step(i, carry):
            h, b = i // blocks, lax.rem(i, blocks)
            lanes = pl.ds(pl.multiple_of(h * HD, HD), HD)
            rows = pl.ds(pl.multiple_of(b * ROWS, ROWS), ROWS)
            out[rows, lanes] = attend(dot_t(q[rows, lanes], k[:, lanes]), v[:, lanes])
            return carry

        lax.fori_loop(first, last, step, 0)

    def give_back(c):
        wait(yback[c], br.at[c])
        unpack(c)
        across(rsend[c], rback[c], rs.at[c], rr.at[c])

    def merge(c):
        wait(rback[c], rr.at[c])
        cls = lax.rem(my_class + CHUNKS - c, CHUNKS)

        def step(w, carry):
            rows = pl.ds(pl.multiple_of((w * CHUNKS + cls) * part, part), part)
            for h in range(heads):
                lanes = slice(h * HD, (h + 1) * HD)
                got = rback[c][w, table[SLOT + h]]
                out[rows, lanes] = jnp.where(flags[h, 0:1, :] == 1, got, out[rows, lanes])
            return carry

        lax.fori_loop(0, W, step, 0)

    fill = heads * blocks // (CHUNKS + 1)

    def stage(st, carry):
        spatial(st * fill, (st + 1) * fill)
        for c in range(CHUNKS):

            @pl.when(st == c)
            def _():
                for p in range(COUNT):
                    if PIECES[p][0] == c:
                        wait(xrecv[p], xr.at[p])
                        compact(p)
                        forward(p)

        return carry

    def launch(p):
        across(xsend[p], xrecv[p], xs.at[p], xr.at[p])

    pack(0)
    pl.semaphore_wait(barrier, frames + W - 2)
    launch(0)
    for p in range(1, COUNT):
        pack(p)
        launch(p)
    lax.fori_loop(0, CHUNKS + 1, stage, 0)
    wait(yrecv, yr)
    temporal()
    backward()
    give_back(0)
    give_back(1)
    give_back(2)
    merge(0)
    merge(1)
    give_back(3)
    merge(2)
    merge(3)
    for p in range(COUNT):
        wait(xsend[p].at[pl.ds(0, W - 1)], xs.at[p])
    for c in range(CHUNKS):
        wait(rsend[c].at[pl.ds(0, W - 1)], rs.at[c])
    wait(yrecv.at[pl.ds(0, frames - 1)], ys)
    wait(result.at[pl.ds(0, frames - 1)], bs)


def attention(n, index, table, flags, q, k, v):
    pos, width = q.shape
    heads = width // HD
    frames = Y * Z
    part = pos // (W * CHUNKS)
    half = n // 2
    vmem = pl.BlockSpec(memory_space=pltpu.VMEM)

    def buffers(count, *shape):
        return [pltpu.VMEM(shape, jnp.bfloat16)] * count

    one, each = pltpu.SemaphoreType.DMA, pltpu.SemaphoreType.DMA((CHUNKS,))
    return pl.pallas_call(
        functools.partial(kernel, n, heads),
        out_shape=jax.ShapeDtypeStruct((pos, width), jnp.bfloat16),
        in_specs=[pl.BlockSpec(memory_space=pltpu.SMEM), vmem, vmem, vmem, vmem],
        out_specs=vmem,
        scratch_shapes=[
            *(pltpu.VMEM((W, SLOTS, b - a, part, HD), jnp.bfloat16) for _, a, b in PIECES),
            *(pltpu.VMEM((W * SLOTS, b - a, part, HD), jnp.bfloat16) for _, a, b in PIECES),
            *(pltpu.VMEM((Y, n, b - a, GROUP, HD), jnp.bfloat16) for _, a, b in PIECES),
            *buffers(1, frames, half, 3, GROUP, HD),
            *buffers(1, frames, half, GROUP, HD),
            *buffers(CHUNKS, Y, n, GROUP, HD),
            *buffers(CHUNKS, W, SLOTS, part, HD),
            *buffers(CHUNKS, W, SLOTS, part, HD),
            pltpu.SemaphoreType.DMA((COUNT,)),
            pltpu.SemaphoreType.DMA((COUNT,)),
            one,
            one,
            one,
            each,
            each,
            each,
        ],
        compiler_params=pltpu.CompilerParams(
            collective_id=2 + index, has_side_effects=True, vmem_limit_bytes=60 << 20
        ),
        name=f"attention_{n}",
    )(table, flags, q, k, v)


def direct_kernel(frames, heads, table, flags, q, k, v, out, send, recv, result, back, ssem, rsem, ssem2, rsem2):
    me = lax.axis_index("frames")
    wsh = lax.axis_index("wshard")
    pos = q.shape[0]
    part = pos // frames
    peers = frames - 1

    def peer(step):
        return lax.rem(me + step, frames)

    barrier = pltpu.get_barrier_semaphore()

    def greet(step, carry):
        pl.semaphore_signal(barrier, inc=1, device_id=(peer(step), wsh), device_id_type=MESH)
        return carry

    lax.fori_loop(1, frames, greet, 0)

    def pack(s):
        lanes = pl.ds(table[HEAD + s] * HD, HD)
        for u, ref in enumerate((q, k, v)):
            send[s, :, u] = ref[:, lanes].reshape(frames, part, HD)
        recv[s, me] = send[s, me]

    def forward(s):
        def step(o, carry):
            to = peer(o)
            pltpu.make_async_remote_copy(
                src_ref=send.at[s, to],
                dst_ref=recv.at[s, me],
                send_sem=ssem.at[s],
                recv_sem=rsem.at[s],
                device_id=(to, wsh),
                device_id_type=MESH,
            ).start()
            return carry

        lax.fori_loop(1, frames, step, 0)

    def backward(s):
        def step(o, carry):
            to = peer(o)
            pltpu.make_async_remote_copy(
                src_ref=result.at[s, to],
                dst_ref=back.at[s, me],
                send_sem=ssem2.at[s],
                recv_sem=rsem2.at[s],
                device_id=(to, wsh),
                device_id_type=MESH,
            ).start()
            return carry

        lax.fori_loop(1, frames, step, 0)

    def wait_all(ref, s, sem):
        some = ref.at[s, pl.ds(0, peers)]
        pltpu.make_async_copy(some, some, sem.at[s]).wait()

    wide = frames * GROUP
    mask = lax.rem(lax.broadcasted_iota(jnp.int32, (wide, wide), 0), GROUP) == lax.rem(
        lax.broadcasted_iota(jnp.int32, (wide, wide), 1), GROUP
    )

    def temporal(s):
        def step(g, carry):
            rows = pl.ds(pl.multiple_of(g * GROUP, GROUP), GROUP)
            qg = recv[s, :, 0, rows, :].reshape(wide, HD)
            kg = recv[s, :, 1, rows, :].reshape(wide, HD)
            vg = recv[s, :, 2, rows, :].reshape(wide, HD)
            scores = jnp.where(mask, dot_t(qg, kg), -jnp.inf)
            result[s, :, rows, :] = attend(scores, vg).reshape(frames, GROUP, HD)
            return carry

        lax.fori_loop(0, part // GROUP, step, 0)
        back[s, me] = result[s, me]

    blocks = pos // ROWS

    def spatial(first, last):
        def step(i, carry):
            h, b = i // blocks, lax.rem(i, blocks)
            lanes = pl.ds(pl.multiple_of(h * HD, HD), HD)
            rows = pl.ds(pl.multiple_of(b * ROWS, ROWS), ROWS)
            out[rows, lanes] = attend(dot_t(q[rows, lanes], k[:, lanes]), v[:, lanes])
            return carry

        lax.fori_loop(first * blocks, last * blocks, step, 0)

    pack(0)
    pl.semaphore_wait(barrier, peers)
    forward(0)
    for s in range(1, SLOTS):
        pack(s)
        forward(s)
    cuts = (0, 2, 4, heads)
    for s in range(SLOTS):
        spatial(cuts[s], cuts[s + 1])
        wait_all(recv, s, rsem)
        temporal(s)
        backward(s)
    for s in range(SLOTS):
        wait_all(send, s, ssem)
        wait_all(result, s, ssem2)
        wait_all(back, s, rsem2)
    for h in range(heads):
        lanes = slice(h * HD, (h + 1) * HD)
        got = back[table[SLOT + h]].reshape(pos, HD)
        out[:, lanes] = jnp.where(flags[h, 0:1, :] == 1, got, out[:, lanes])


def direct(table, flags, q, k, v):
    pos, width = q.shape
    frames = Y * Z
    part = pos // frames
    vmem = pl.BlockSpec(memory_space=pltpu.VMEM)
    sems = pltpu.SemaphoreType.DMA((SLOTS,))
    return pl.pallas_call(
        functools.partial(direct_kernel, frames, width // HD),
        out_shape=jax.ShapeDtypeStruct((pos, width), jnp.bfloat16),
        in_specs=[pl.BlockSpec(memory_space=pltpu.SMEM), vmem, vmem, vmem, vmem],
        out_specs=vmem,
        scratch_shapes=[
            pltpu.VMEM((SLOTS, frames, 3, part, HD), jnp.bfloat16),
            pltpu.VMEM((SLOTS, frames, 3, part, HD), jnp.bfloat16),
            pltpu.VMEM((SLOTS, frames, part, HD), jnp.bfloat16),
            pltpu.VMEM((SLOTS, frames, part, HD), jnp.bfloat16),
            sems,
            sems,
            sems,
            sems,
        ],
        compiler_params=pltpu.CompilerParams(
            collective_id=0, has_side_effects=True, vmem_limit_bytes=60 << 20
        ),
        name="attention_direct",
    )(table, flags, q, k, v)


def body(queries, keys, values, labels):
    _, pos, width = queries.shape
    heads = width // HD
    table, flags, which = make_table(share(labels), heads)
    branches = [functools.partial(attention, n, i) for i, n in enumerate(SIZES)] + [direct]
    q, k, v = (a.reshape(pos, width) for a in (queries, keys, values))
    out = lax.switch(which.reshape(()), branches, table, flags, q, k, v)
    return out.reshape(1, pos, width)


def solution(mesh):
    spec = P("frames", None, "wshard")
    return jax.shard_map(
        body,
        mesh=mesh,
        in_specs=(spec, spec, spec, P("wshard")),
        out_specs=spec,
        check_vma=False,
    )
```

```python
import functools

import jax
import jax.numpy as jnp
from jax import lax
from jax.experimental import pallas as pl
from jax.experimental.pallas import tpu as pltpu
from jax.sharding import PartitionSpec as P

HD = 128
SLOTS = 3
GROUP = 16
ROWS = 256
CHUNKS = 4
FIRST = 5
Y, Z, W = 4, 8, 8
COEF = HD ** (-0.5) * 1.4426950408889634
MESH = pl.DeviceIdType.MESH
SIZES = (10, 12, 14, 16, 18)
PIECES = ((0, 0, 1), (0, 1, 2), (0, 2, 3), (1, 0, 3), (2, 0, 3), (3, 0, 3))
COUNT = len(PIECES)
HEAD, SLOT, SOURCE, PLACE, TABLE = 0, 8, 16, 48, 128


def dot_t(a, b):
    return lax.dot_general(a, b, (((1,), (1,)), ((), ())), preferred_element_type=jnp.float32)


def attend(scores, vals):
    top = jnp.max(scores, axis=-1, keepdims=True)
    expo = jnp.exp2((scores - top) * COEF)
    total = jnp.sum(expo, axis=-1, keepdims=True)
    out = jnp.dot(expo.astype(jnp.bfloat16), vals, preferred_element_type=jnp.float32)
    return (out / total).astype(jnp.bfloat16)


def share_kernel(heads, labels, every, mine, ssem, rsem):
    fr = lax.axis_index("frames")
    me = lax.axis_index("wshard")
    barrier = pltpu.get_barrier_semaphore()
    for o in range(1, W):
        to = (fr, lax.rem(me + o, W))
        pl.semaphore_signal(barrier, inc=1, device_id=to, device_id_type=MESH)
    lane = lax.broadcasted_iota(jnp.int32, (8, HD), 1)
    row = jnp.zeros((8, HD), jnp.int32)
    for h in range(heads):
        row += (lane == h).astype(jnp.int32) * labels[h]
    mine[...] = row
    every[me] = row
    pl.semaphore_wait(barrier, W - 1)
    for o in range(1, W):
        pltpu.make_async_remote_copy(
            src_ref=mine,
            dst_ref=every.at[me],
            send_sem=ssem,
            recv_sem=rsem,
            device_id=(fr, lax.rem(me + o, W)),
            device_id_type=MESH,
        ).start()
    some = every.at[pl.ds(0, W - 1)]
    pltpu.make_async_copy(some, some, ssem).wait()
    pltpu.make_async_copy(some, some, rsem).wait()


def share(labels):
    return pl.pallas_call(
        functools.partial(share_kernel, labels.shape[0]),
        out_shape=jax.ShapeDtypeStruct((W, 8, HD), jnp.int32),
        in_specs=[pl.BlockSpec(memory_space=pltpu.SMEM)],
        out_specs=pl.BlockSpec(memory_space=pltpu.VMEM),
        scratch_shapes=[
            pltpu.VMEM((8, HD), jnp.int32),
            pltpu.SemaphoreType.DMA,
            pltpu.SemaphoreType.DMA,
        ],
        compiler_params=pltpu.CompilerParams(collective_id=1, has_side_effects=True),
        name="share_labels",
    )(labels)


def table_kernel(heads, every, table, flags, which):
    me = lax.axis_index("wshard")
    for i in range(TABLE):
        table[i] = 0
    total = jnp.int32(0)
    for w in range(W):
        slot = jnp.int32(0)
        for h in range(heads):
            table[SOURCE + total] = w * SLOTS + slot
            table[PLACE + w * SLOTS + slot] = total
            label = every[w, 0, h]
            total += label
            slot += label
    last = total - 1
    for i in range(W * SLOTS):
        table[PLACE + i] = jnp.minimum(table[PLACE + i], last)
    for i in range(SLOTS, 32):
        table[SOURCE + i] = jnp.where(i < total, table[SOURCE + i], 0)
    branch = jnp.int32(0)
    for size in SIZES:
        branch += (total > size).astype(jnp.int32)
    which[0] = branch
    slot = jnp.int32(0)
    for h in range(heads):
        label = every[me, 0, h]
        table[HEAD + slot] = h
        table[SLOT + h] = jnp.minimum(slot, SLOTS - 1)
        slot += label
        flags[h] = jnp.full((8, HD), label, jnp.int32)


def make_table(every, heads):
    return pl.pallas_call(
        functools.partial(table_kernel, heads),
        out_shape=(
            jax.ShapeDtypeStruct((TABLE,), jnp.int32),
            jax.ShapeDtypeStruct((heads, 8, HD), jnp.int32),
            jax.ShapeDtypeStruct((1,), jnp.int32),
        ),
        in_specs=[pl.BlockSpec(memory_space=pltpu.SMEM)],
        out_specs=(
            pl.BlockSpec(memory_space=pltpu.SMEM),
            pl.BlockSpec(memory_space=pltpu.VMEM),
            pl.BlockSpec(memory_space=pltpu.SMEM),
        ),
        name="make_table",
    )(every)


def kernel(n, heads, table, flags, q_hbm, k_hbm, v_hbm, out, q, k, v, ls, *scratch):
    scratch = list(scratch)
    for u, (src, dst) in enumerate(((q_hbm, q), (k_hbm, k), (v_hbm, v))):
        pltpu.make_async_copy(src, dst, ls.at[u]).start()

    def take(count):
        some = scratch[:count]
        del scratch[:count]
        return some

    xsend, xrecv, ysend = take(COUNT), take(COUNT), take(COUNT)
    yrecv, result = take(2)
    yback, rsend, rback = take(CHUNKS), take(CHUNKS), take(CHUNKS)
    xs, xr, ys, yr, bs, br, rs, rr = scratch
    fr = lax.axis_index("frames")
    wsh = lax.axis_index("wshard")
    frames = Y * Z
    pos = q.shape[0]
    part = pos // (W * CHUNKS)
    half = n // 2
    cut = (half + 1) // 2
    parts = ((0, cut), (cut, half))
    my_y, my_z = fr // Z, lax.rem(fr, Z)
    my_class = lax.rem(my_y + my_z, CHUNKS)
    my_half = my_z // CHUNKS

    def peer(step):
        return lax.rem(fr + step, frames)

    barrier = pltpu.get_barrier_semaphore()

    def greet(step, carry):
        pl.semaphore_signal(barrier, inc=1, device_id=(peer(step), wsh), device_id_type=MESH)
        return carry

    for o in range(1, W):
        to = (fr, lax.rem(wsh + o, W))
        pl.semaphore_signal(barrier, inc=1, device_id=to, device_id_type=MESH)
    lax.fori_loop(1, frames, greet, 0)

    def remote(src, dst, send_sem, recv_sem, to):
        pltpu.make_async_remote_copy(
            src_ref=src,
            dst_ref=dst,
            send_sem=send_sem,
            recv_sem=recv_sem,
            device_id=to,
            device_id_type=MESH,
        ).start()

    def wait(some, sem):
        pltpu.make_async_copy(some, some, sem).wait()

    def pack(p):
        c, first, last = PIECES[p]
        cls = lax.rem(my_class + c, CHUNKS)

        def step(w, carry):
            rows = pl.ds(pl.multiple_of((w * CHUNKS + cls) * part, part), part)
            for s in range(SLOTS):
                lanes = pl.ds(table[HEAD + s] * HD, HD)
                for u in range(first, last):
                    xsend[p][w, s, u - first] = (q, k, v)[u][rows, lanes]
            return carry

        lax.fori_loop(0, W, step, 0)

    def across(src, dst, send_sem, recv_sem):
        mine = dst.at[wsh] if dst.shape[0] == W else dst.at[pl.ds(wsh * SLOTS, SLOTS)]
        pltpu.make_async_copy(src.at[wsh], mine, recv_sem).start()
        for o in range(1, W):
            to = lax.rem(wsh + o, W)
            remote(src.at[to], mine, send_sem, recv_sem, (fr, to))

    def compact(p):
        def step(i, carry):
            source = table[SOURCE + i]
            block = xrecv[p][source]
            for y in range(Y):
                ysend[p][y, i] = block[:, y * GROUP : (y + 1) * GROUP]
            return carry

        lax.fori_loop(0, n, step, 0)

    def forward(p, lo, hi, sem):
        c, first, last = PIECES[p]
        cls = lax.rem(my_class + c, CHUNKS)

        def step(e, carry):
            y = lax.rem(e // 2 + my_y, Y)
            b = lax.rem(e + my_half, 2)
            to = y * Z + lax.rem(cls + CHUNKS - y, CHUNKS) + CHUNKS * b
            src = ysend[p].at[y, pl.ds(b * half + lo, hi - lo)]
            dst = yrecv.at[fr, pl.ds(lo, hi - lo), pl.ds(first, last - first)]
            if c:
                remote(src, dst, ys, sem, (to, wsh))
                return carry

            @pl.when(to == fr)
            def _():
                pltpu.make_async_copy(src, dst, sem).start()

            @pl.when(to != fr)
            def _():
                remote(src, dst, ys, sem, (to, wsh))

            return carry

        lax.fori_loop(0, 2 * Y, step, 0)

    wide = frames * GROUP
    mask = lax.rem(lax.broadcasted_iota(jnp.int32, (wide, wide), 0), GROUP) == lax.rem(
        lax.broadcasted_iota(jnp.int32, (wide, wide), 1), GROUP
    )

    def temporal(lo, hi):
        def step(j, carry):
            qg = yrecv[:, j, 0].reshape(wide, HD)
            kg = yrecv[:, j, 1].reshape(wide, HD)
            vg = yrecv[:, j, 2].reshape(wide, HD)
            scores = jnp.where(mask, dot_t(qg, kg), -jnp.inf)
            result[:, j] = attend(scores, vg).reshape(frames, GROUP, HD)
            return carry

        lax.fori_loop(lo, hi, step, 0)

    def backward(lo, hi):
        for c in range(CHUNKS):
            dst = yback[c].at[my_y, pl.ds(my_half * half + lo, hi - lo)]
            cls = lax.rem(my_class + c, CHUNKS)

            def step(e, carry):
                y = lax.rem(e // 2 + my_y, Y)
                b = lax.rem(e + my_half, 2)
                to = y * Z + lax.rem(cls + CHUNKS - y, CHUNKS) + CHUNKS * b
                src = result.at[to, pl.ds(lo, hi - lo)]
                if c:
                    remote(src, dst, bs, br.at[c], (to, wsh))
                    return carry

                @pl.when(to == fr)
                def _():
                    pltpu.make_async_copy(src, dst, br.at[c]).start()

                @pl.when(to != fr)
                def _():
                    remote(src, dst, bs, br.at[c], (to, wsh))

                return carry

            lax.fori_loop(0, 2 * Y, step, 0)

    def unpack(c):
        def step(w, carry):
            for s in range(SLOTS):
                place = table[PLACE + w * SLOTS + s]
                rsend[c][w, s] = yback[c][:, place].reshape(part, HD)
            return carry

        lax.fori_loop(0, W, step, 0)

    blocks = pos // ROWS

    def spatial(first, last):
        def step(i, carry):
            h, b = i // blocks, lax.rem(i, blocks)
            lanes = pl.ds(pl.multiple_of(h * HD, HD), HD)
            rows = pl.ds(pl.multiple_of(b * ROWS, ROWS), ROWS)
            out[rows, lanes] = attend(dot_t(q[rows, lanes], k[:, lanes]), v[:, lanes])
            return carry

        lax.fori_loop(first, last, step, 0)

    def give_back(c):
        wait(yback[c], br.at[c])
        unpack(c)
        across(rsend[c], rback[c], rs.at[c], rr.at[c])

    def merge(c):
        wait(rback[c], rr.at[c])
        cls = lax.rem(my_class + CHUNKS - c, CHUNKS)

        def step(w, carry):
            rows = pl.ds(pl.multiple_of((w * CHUNKS + cls) * part, part), part)
            for h in range(heads):
                lanes = slice(h * HD, (h + 1) * HD)
                got = rback[c][w, table[SLOT + h]]
                out[rows, lanes] = jnp.where(flags[h, 0:1, :] == 1, got, out[rows, lanes])
            return carry

        lax.fori_loop(0, W, step, 0)

    last_block = heads * blocks
    fill = (last_block + FIRST) // (CHUNKS + 1)

    def stage(st, carry):
        begun = (st + CHUNKS) // (CHUNKS + 1)
        spatial(st * fill - FIRST * begun, (st + 1) * fill - FIRST)
        for c in range(CHUNKS):

            @pl.when(st == c)
            def _():
                for p in range(COUNT):
                    if PIECES[p][0] == c:
                        wait(xrecv[p], xr.at[p])
                        compact(p)
                        if c < CHUNKS - 1:
                            forward(p, 0, half, yr.at[2])
                        else:
                            for i, (lo, hi) in enumerate(parts):
                                forward(p, lo, hi, yr.at[i])

        return carry

    def launch(p):
        across(xsend[p], xrecv[p], xs.at[p], xr.at[p])

    def loaded(u):
        pltpu.make_async_copy((q_hbm, k_hbm, v_hbm)[u], (q, k, v)[u], ls.at[u]).wait()

    loaded(0)
    pack(0)
    pl.semaphore_wait(barrier, frames + W - 2)
    launch(0)
    for p in range(1, COUNT):
        if p < 3:
            loaded(p)
        pack(p)
        launch(p)
    lax.fori_loop(0, CHUNKS + 1, stage, 0)
    wait(yrecv.at[pl.ds(0, frames - 2 * Y)], yr.at[2])
    for i, (lo, hi) in enumerate(parts):
        wait(yrecv.at[pl.ds(0, 2 * Y), pl.ds(lo, hi - lo)], yr.at[i])
        temporal(lo, hi)
        backward(lo, hi)
    give_back(0)
    give_back(1)
    give_back(2)
    merge(0)
    merge(1)
    give_back(3)
    merge(2)
    merge(3)
    for p in range(COUNT):
        wait(xsend[p].at[pl.ds(0, W - 1)], xs.at[p])
    for c in range(CHUNKS):
        wait(rsend[c].at[pl.ds(0, W - 1)], rs.at[c])
    wait(yrecv.at[pl.ds(0, frames - 1)], ys)
    wait(result.at[pl.ds(0, frames - 1)], bs)


def attention(n, index, table, flags, q, k, v):
    pos, width = q.shape
    heads = width // HD
    frames = Y * Z
    part = pos // (W * CHUNKS)
    half = n // 2
    hbm = pl.BlockSpec(memory_space=pl.ANY)
    vmem = pl.BlockSpec(memory_space=pltpu.VMEM)

    def buffers(count, *shape):
        return [pltpu.VMEM(shape, jnp.bfloat16)] * count

    one, each = pltpu.SemaphoreType.DMA, pltpu.SemaphoreType.DMA((CHUNKS,))
    return pl.pallas_call(
        functools.partial(kernel, n, heads),
        out_shape=jax.ShapeDtypeStruct((pos, width), jnp.bfloat16),
        in_specs=[pl.BlockSpec(memory_space=pltpu.SMEM), vmem, hbm, hbm, hbm],
        out_specs=vmem,
        scratch_shapes=[
            *buffers(3, pos, width),
            pltpu.SemaphoreType.DMA((3,)),
            *(pltpu.VMEM((W, SLOTS, b - a, part, HD), jnp.bfloat16) for _, a, b in PIECES),
            *(pltpu.VMEM((W * SLOTS, b - a, part, HD), jnp.bfloat16) for _, a, b in PIECES),
            *(pltpu.VMEM((Y, n, b - a, GROUP, HD), jnp.bfloat16) for _, a, b in PIECES),
            *buffers(1, frames, half, 3, GROUP, HD),
            *buffers(1, frames, half, GROUP, HD),
            *buffers(CHUNKS, Y, n, GROUP, HD),
            *buffers(CHUNKS, W, SLOTS, part, HD),
            *buffers(CHUNKS, W, SLOTS, part, HD),
            pltpu.SemaphoreType.DMA((COUNT,)),
            pltpu.SemaphoreType.DMA((COUNT,)),
            one,
            pltpu.SemaphoreType.DMA((3,)),
            one,
            each,
            each,
            each,
        ],
        compiler_params=pltpu.CompilerParams(
            collective_id=2 + index, has_side_effects=True, vmem_limit_bytes=60 << 20
        ),
        name=f"attention_{n}",
    )(table, flags, q, k, v)


def direct_kernel(frames, heads, table, flags, q, k, v, out, send, recv, result, back, ssem, rsem, ssem2, rsem2):
    me = lax.axis_index("frames")
    wsh = lax.axis_index("wshard")
    pos = q.shape[0]
    part = pos // frames
    peers = frames - 1

    def peer(step):
        return lax.rem(me + step, frames)

    barrier = pltpu.get_barrier_semaphore()

    def greet(step, carry):
        pl.semaphore_signal(barrier, inc=1, device_id=(peer(step), wsh), device_id_type=MESH)
        return carry

    lax.fori_loop(1, frames, greet, 0)

    def pack(s):
        lanes = pl.ds(table[HEAD + s] * HD, HD)
        for u, ref in enumerate((q, k, v)):
            send[s, :, u] = ref[:, lanes].reshape(frames, part, HD)
        recv[s, me] = send[s, me]

    def forward(s):
        def step(o, carry):
            to = peer(o)
            pltpu.make_async_remote_copy(
                src_ref=send.at[s, to],
                dst_ref=recv.at[s, me],
                send_sem=ssem.at[s],
                recv_sem=rsem.at[s],
                device_id=(to, wsh),
                device_id_type=MESH,
            ).start()
            return carry

        lax.fori_loop(1, frames, step, 0)

    def backward(s):
        def step(o, carry):
            to = peer(o)
            pltpu.make_async_remote_copy(
                src_ref=result.at[s, to],
                dst_ref=back.at[s, me],
                send_sem=ssem2.at[s],
                recv_sem=rsem2.at[s],
                device_id=(to, wsh),
                device_id_type=MESH,
            ).start()
            return carry

        lax.fori_loop(1, frames, step, 0)

    def wait_all(ref, s, sem):
        some = ref.at[s, pl.ds(0, peers)]
        pltpu.make_async_copy(some, some, sem.at[s]).wait()

    wide = frames * GROUP
    mask = lax.rem(lax.broadcasted_iota(jnp.int32, (wide, wide), 0), GROUP) == lax.rem(
        lax.broadcasted_iota(jnp.int32, (wide, wide), 1), GROUP
    )

    def temporal(s):
        def step(g, carry):
            rows = pl.ds(pl.multiple_of(g * GROUP, GROUP), GROUP)
            qg = recv[s, :, 0, rows, :].reshape(wide, HD)
            kg = recv[s, :, 1, rows, :].reshape(wide, HD)
            vg = recv[s, :, 2, rows, :].reshape(wide, HD)
            scores = jnp.where(mask, dot_t(qg, kg), -jnp.inf)
            result[s, :, rows, :] = attend(scores, vg).reshape(frames, GROUP, HD)
            return carry

        lax.fori_loop(0, part // GROUP, step, 0)
        back[s, me] = result[s, me]

    blocks = pos // ROWS

    def spatial(first, last):
        def step(i, carry):
            h, b = i // blocks, lax.rem(i, blocks)
            lanes = pl.ds(pl.multiple_of(h * HD, HD), HD)
            rows = pl.ds(pl.multiple_of(b * ROWS, ROWS), ROWS)
            out[rows, lanes] = attend(dot_t(q[rows, lanes], k[:, lanes]), v[:, lanes])
            return carry

        lax.fori_loop(first * blocks, last * blocks, step, 0)

    pack(0)
    pl.semaphore_wait(barrier, peers)
    forward(0)
    for s in range(1, SLOTS):
        pack(s)
        forward(s)
    cuts = (0, 2, 4, heads)
    for s in range(SLOTS):
        spatial(cuts[s], cuts[s + 1])
        wait_all(recv, s, rsem)
        temporal(s)
        backward(s)
    for s in range(SLOTS):
        wait_all(send, s, ssem)
        wait_all(result, s, ssem2)
        wait_all(back, s, rsem2)
    for h in range(heads):
        lanes = slice(h * HD, (h + 1) * HD)
        got = back[table[SLOT + h]].reshape(pos, HD)
        out[:, lanes] = jnp.where(flags[h, 0:1, :] == 1, got, out[:, lanes])


def direct(table, flags, q, k, v):
    pos, width = q.shape
    frames = Y * Z
    part = pos // frames
    vmem = pl.BlockSpec(memory_space=pltpu.VMEM)
    sems = pltpu.SemaphoreType.DMA((SLOTS,))
    return pl.pallas_call(
        functools.partial(direct_kernel, frames, width // HD),
        out_shape=jax.ShapeDtypeStruct((pos, width), jnp.bfloat16),
        in_specs=[pl.BlockSpec(memory_space=pltpu.SMEM), vmem, vmem, vmem, vmem],
        out_specs=vmem,
        scratch_shapes=[
            pltpu.VMEM((SLOTS, frames, 3, part, HD), jnp.bfloat16),
            pltpu.VMEM((SLOTS, frames, 3, part, HD), jnp.bfloat16),
            pltpu.VMEM((SLOTS, frames, part, HD), jnp.bfloat16),
            pltpu.VMEM((SLOTS, frames, part, HD), jnp.bfloat16),
            sems,
            sems,
            sems,
            sems,
        ],
        compiler_params=pltpu.CompilerParams(
            collective_id=0, has_side_effects=True, vmem_limit_bytes=60 << 20
        ),
        name="attention_direct",
    )(table, flags, q, k, v)


def body(queries, keys, values, labels):
    _, pos, width = queries.shape
    heads = width // HD
    table, flags, which = make_table(share(labels), heads)
    branches = [functools.partial(attention, n, i) for i, n in enumerate(SIZES)] + [direct]
    q, k, v = (a.reshape(pos, width) for a in (queries, keys, values))
    out = lax.switch(which.reshape(()), branches, table, flags, q, k, v)
    return out.reshape(1, pos, width)


def solution(mesh):
    spec = P("frames", None, "wshard")
    return jax.shard_map(
        body,
        mesh=mesh,
        in_specs=(spec, spec, spec, P("wshard")),
        out_specs=spec,
        check_vma=False,
    )
```
